32 devices in a mesh: gx: 4 (over y, core), gy: 4 (over z), gz: 2 (over x).
Axes of the slice: x: 2, y: 2, z: 4, core: 2. Of those that a mesh axis runs over, the one named last changes fastest.
Arguments:
- concentration: float32 [192, 64, 256], P('gx', 'gy', 'gz'), may hold values from -6 to 6
- dispersion: float32 [192, 64, 256], P('gx', 'gy', 'gz'), may hold values from 0.2 to 1.2
- disp_step: float32 [192, 64, 256], P('gx', 'gy', 'gz'), may hold values from -6 to 6
- capacity: float32 [192, 64, 256], P('gx', 'gy', 'gz'), may hold values from 1 to 4
- cap_step: float32 [192, 64, 256], P('gx', 'gy', 'gz'), may hold values from -6 to 6
- velocity: float32 [192, 64, 256], P('gx', 'gy', 'gz'), may hold values from 0.2 to 1
- voxel_mask: int32 [24, 8, 32], P('gx', 'gy', 'gz'), may hold values 0 or 1
- voxel_class: int32 [24, 8, 32], P('gx', 'gy', 'gz'), may hold values from 0 to 3
- class_weight: float32 [4], replicated, may hold values from 4 to 40
Outputs:
- grad_dispersion: float32 [192, 64, 256], P('gx', 'gy', 'gz')
- grad_capacity: float32 [192, 64, 256], P('gx', 'gy', 'gz')
The draws below stay inside these ranges and needn't reach their ends.
All inputs are finite; a program needn't handle non-finite values. No bound on the sum of `voxel_mask` on one device may be relied on, other than what follows from the above.
Results may differ from the reference program's by a relative error of at most 0.00024.
Values sent between devices are 32-bit elements; how exact they have to be, the bound alone decides.
A program may use at most 64 MiB of HBM per device.

```python
import math
import jax
import jax.numpy as jnp
from jax import lax

CLASSES = 4
NX = 192
NY = 64
NZ = 256
MX = 24
MY = 8
MZ = 32


def set_ends(drawn, rng, least, largest):
    dims = drawn.shape
    spot = [jax.random.randint(jax.random.fold_in(rng, axis), (), 0, dims[axis]) for axis in range(len(dims))]
    drawn = drawn.at[tuple(spot)].set(least)
    longest = dims.index(max(dims))
    spot[longest] = (spot[longest] + 1) % dims[longest]
    return drawn.at[tuple(spot)].set(largest)


def steps_of(own_key, dims, split, low, largest):
    level = 1.0
    for position, blocks in split:
        heights = jax.random.uniform(jax.random.fold_in(jax.random.fold_in(own_key, 6), position), (blocks,), jnp.float32, low / len(split), largest / len(split))
        level = level * jnp.repeat(jnp.exp(heights), dims[position] // blocks).reshape((-1,) + (1,) * (len(dims) - 1 - position))
    return level


def centred(own_key, extent, deviation, limit, shards=(), held_as=jnp.bfloat16):
    values = jax.random.normal(own_key, extent, jnp.float32) * deviation
    if len(shards) > 0:
        values = steps_of(own_key, extent, shards, -0.22, 0.18) * values
    return jnp.clip(values, min=-limit, max=limit).astype(held_as)


def setup_inputs(seed: int = 0) -> dict:
    arg_keys = jax.random.split(jax.random.key(seed), 10)
    return {
        "concentration": centred(arg_keys[0], (NX, NY, NZ), 1.0, 6.0, ((0, 4), (1, 4), (2, 2)), jnp.float32),
        "dispersion": jnp.clip(0.2 + 1 * jax.random.uniform(arg_keys[1], (NX, NY, NZ), jnp.float32) ** steps_of(arg_keys[1], (NX, NY, NZ), ((0, 4), (1, 4), (2, 2)), -0.2, 0.2), 0.2, 1.2),
        "disp_step": centred(arg_keys[2], (NX, NY, NZ), 1.0, 6.0, ((0, 4), (1, 4), (2, 2)), jnp.float32),
        "capacity": jnp.clip(1.0 + 3.0 * jax.random.uniform(arg_keys[3], (NX, NY, NZ), jnp.float32) ** steps_of(arg_keys[3], (NX, NY, NZ), ((0, 4), (1, 4), (2, 2)), -0.2, 0.2), 1.0, 4.0),
        "cap_step": centred(arg_keys[4], (NX, NY, NZ), 1.0, 6.0, ((0, 4), (1, 4), (2, 2)), jnp.float32),
        "velocity": jnp.clip(0.2 + 0.8 * jax.random.uniform(arg_keys[5], (NX, NY, NZ), jnp.float32) ** steps_of(arg_keys[5], (NX, NY, NZ), ((0, 4), (1, 4), (2, 2)), -0.2, 0.2), 0.2, 1.0),
        "voxel_mask": set_ends((jax.random.randint(arg_keys[6], (MX, MY, MZ), 0, 4) < 3).astype(jnp.int32), jax.random.fold_in(arg_keys[6], 1), 0, 1),
        "voxel_class": set_ends(jax.random.randint(arg_keys[7], (MX, MY, MZ), 0, CLASSES), jax.random.fold_in(arg_keys[7], 1), 0, CLASSES - 1).astype(jnp.int32),
        "class_weight": jnp.clip(jnp.exp(jax.random.uniform(arg_keys[8], (CLASSES,), jnp.float32, math.log(4.0), math.log(40.0))), 4.0, 40.0),
    }


time_step = 0.1

def sides(padded):
    return [padded[2:, 1:-1, 1:-1], padded[:-2, 1:-1, 1:-1], padded[1:-1, 2:, 1:-1], padded[1:-1, :-2, 1:-1], padded[1:-1, 1:-1, 2:], padded[1:-1, 1:-1, :-2]]

def inner(padded):
    return padded[1:-1, 1:-1, 1:-1]

def diffuse(field_pad, coef_pad):
    center = inner(field_pad)
    coef = inner(coef_pad)
    total = jnp.zeros(center.shape, jnp.float32)
    for near_field, near_coef in zip(sides(field_pad), sides(coef_pad)):
        total = total + 0.5 * (coef + near_coef) * (near_field - center)
    return total

def advect(field_pad, vel_pad):
    return vel_pad[1:-1, 1:-1, :-2] * field_pad[1:-1, 1:-1, :-2] - inner(vel_pad) * inner(field_pad)

def advect_back(field_pad, vel_center):
    return vel_center * (field_pad[1:-1, 1:-1, 2:] - inner(field_pad))

def face_grad(mult_pad, field_pad):
    mult = inner(mult_pad)
    center = inner(field_pad)
    total = jnp.zeros(center.shape, jnp.float32)
    for near_mult, near_field in zip(sides(mult_pad), sides(field_pad)):
        total = total + 0.5 * (mult - near_mult) * (near_field - center)
    return total

def voxel_weights(voxel_mask, voxel_class, class_weight):
    labels = jnp.arange(class_weight.shape[0]).astype(jnp.int32)
    picked = jnp.where(voxel_class[None] == labels[:, None, None, None], class_weight[:, None, None, None], 0.0)
    return voxel_mask.astype(jnp.float32) * lax.optimization_barrier(jnp.sum(picked, axis=0))

def restrict_prolong(final, weights):
    sx, sy, sz = weights.shape
    coarse = final.reshape(sx, 8, sy, 8, sz, 8).mean(axis=(1, 3, 5))
    valued = weights * coarse
    return jnp.broadcast_to(valued[:, None, :, None, :, None], (sx, 8, sy, 8, sz, 8)).reshape(final.shape)

def reference(concentration, dispersion, disp_step, capacity, cap_step, velocity, voxel_mask, voxel_class, class_weight):
    conc_pad = jnp.pad(concentration, 1)
    disp_pad = jnp.pad(dispersion, 1)
    step_pad = jnp.pad(disp_step, 1)
    vel_pad = jnp.pad(velocity, 1)
    first_rate = diffuse(conc_pad, disp_pad) + advect(conc_pad, vel_pad)
    later = concentration + time_step / capacity * first_rate
    tangent = time_step / capacity * diffuse(conc_pad, step_pad) - time_step * cap_step / capacity ** 2 * first_rate
    later_pad = jnp.pad(later, 1)
    tangent_pad = jnp.pad(tangent, 1)
    second_rate = diffuse(later_pad, disp_pad) + advect(later_pad, vel_pad)
    final = tangent + time_step / capacity * (diffuse(tangent_pad, disp_pad) + advect(tangent_pad, vel_pad) + diffuse(later_pad, step_pad)) - time_step * cap_step / capacity ** 2 * second_rate
    weights = voxel_weights(voxel_mask, voxel_class, class_weight)
    source = restrict_prolong(final, weights)
    scaled = time_step * source / capacity
    scaled_pad = jnp.pad(scaled, 1)
    earlier = source + diffuse(scaled_pad, disp_pad) + advect_back(scaled_pad, velocity)
    scaled_first = time_step * earlier / capacity
    first_pad = jnp.pad(scaled_first, 1)
    grad_dispersion = face_grad(scaled_pad, later_pad) + face_grad(first_pad, conc_pad)
    grad_capacity = -scaled * second_rate / capacity - scaled_first * first_rate / capacity
    return (grad_dispersion, grad_capacity)
```

```python
import functools

import jax
import jax.numpy as jnp
from jax import lax
from jax.experimental import pallas as pl
from jax.experimental.pallas import tpu as pltpu
from jax.sharding import PartitionSpec as P

time_step = 0.1
MESH = pl.DeviceIdType.MESH
AXES = ("gx", "gy", "gz")
TOP = 8
EDGE = 8
VOXEL = 8
EXACT = lax.Precision.HIGHEST


def kernel(
    conc, disp, step, vel, cap_in, capstep_in, mask, label, class_weight,
    out_d, out_c,
    f_in, f_mid, f_sc, f_first,
    cap, capstep, ratio, rate1, rate2, part, res_d, res_c,
    ys_in, ys_mid, ys_sc, ys_first,
    yr_in, yr_mid, yr_sc, yr_first,
    zs_in, zs_mid, zs_sc, zs_first,
    zr_in, zr_mid, zr_sc, zr_first,
    coarse, weight, load_sem, out_sem, send_sem, recv_sem,
):
    nx, ny, nz = cap.shape
    rows = ny + 2 * EDGE
    place = [lax.axis_index(a) for a in AXES]
    count = [lax.axis_size(a) for a in AXES]
    has_lo = [p > 0 for p in place]
    has_hi = [p < n - 1 for p, n in zip(place, count)]

    def main(ref):
        return ref.at[pl.ds(1, nx), pl.ds(TOP, ny)]

    loads = []
    for i, (src, dst) in enumerate((
        (conc, main(f_in.at[0])), (disp, main(f_in.at[1])), (step, main(f_in.at[2])),
        (vel, main(f_in.at[3])), (cap_in, cap), (capstep_in, capstep),
    )):
        load = pltpu.make_async_copy(src, dst, load_sem.at[i])
        load.start()
        loads.append(load)

    for ref in (f_in, f_mid, f_sc, f_first):
        for k in range(ref.shape[0]):
            for x in (0, nx + 1):
                ref[k, x, TOP:TOP + ny, :] = jnp.zeros((ny, nz), jnp.float32)
    for ref in (yr_in, yr_mid, yr_sc, yr_first, zr_in, zr_mid, zr_sc, zr_first):
        ref[...] = jnp.zeros(ref.shape, jnp.float32)

    barrier = pltpu.get_barrier_semaphore()
    for a, name in enumerate(AXES):
        @pl.when(has_lo[a])
        def _():
            pl.semaphore_signal(barrier, inc=1, device_id={name: place[a] - 1}, device_id_type=MESH)

        @pl.when(has_hi[a])
        def _():
            pl.semaphore_signal(barrier, inc=1, device_id={name: place[a] + 1}, device_id_type=MESH)

    lane = lax.broadcasted_iota(jnp.int32, (ny, nz), 1)
    first_lane = lane == 0
    last_lane = lane == nz - 1
    pair = lane // 2

    def copies(phase, fields, ys, yr, zs, zr):
        k = yr.shape[1]

        def remote(src, dst, axis, side):
            at = (phase * 3 + axis) * 2 + side
            to = place[axis] - 1 if side == 0 else place[axis] + 1
            return pltpu.make_async_remote_copy(
                src_ref=src, dst_ref=dst, send_sem=send_sem.at[at], recv_sem=recv_sem.at[at],
                device_id={AXES[axis]: to}, device_id_type=MESH)

        def slab(x):
            return fields.at[pl.ds(0, k), x, pl.ds(TOP, ny)]

        return [
            (remote(slab(1), slab(nx + 1), 0, 0), remote(slab(nx), slab(0), 0, 1)),
            (remote(ys.at[0], yr.at[1], 1, 0), remote(ys.at[1], yr.at[0], 1, 1)),
            (remote(zs, zr.at[1], 2, 0), remote(zs, zr.at[0], 2, 1)),
        ]

    def start(pairs, axis):
        lo, hi = pairs[axis]

        @pl.when(has_lo[axis])
        def _():
            lo.start()

        @pl.when(has_hi[axis])
        def _():
            hi.start()

    def finish(pairs):
        for axis in range(3):
            lo, hi = pairs[axis]

            @pl.when(has_lo[axis])
            def _():
                hi.wait_recv()
                lo.wait_send()

            @pl.when(has_hi[axis])
            def _():
                lo.wait_recv()
                hi.wait_send()

    def pack_rows(fields, ys, k):
        flat = fields.reshape(fields.shape[0], (nx + 2) * rows, nz)
        for i in range(k):
            ys[0, i] = flat[i, pl.ds(rows + TOP, nx, stride=rows), :]
            ys[1, i] = flat[i, pl.ds(rows + TOP + ny - 1, nx, stride=rows), :]

    def unpack(fields, yr, zr, k):
        flat = fields.reshape(fields.shape[0], (nx + 2) * rows, nz)
        for i in range(k):
            flat[i, pl.ds(rows + TOP - 1, nx, stride=rows), :] = yr[0, i]
            flat[i, pl.ds(rows + TOP + ny, nx, stride=rows), :] = yr[1, i]
        for i in range(zr.shape[1]):
            above = pltpu.roll(zr[1, i], nz - 1, 1)
            below = pltpu.roll(zr[0, i], 1, 1)
            zr[0, i] = jnp.where(lane % 2 == 0, above, below)

    def pack_column(plane, slab, x):
        return jnp.where(pair == x, pltpu.roll(slab, 2 * x + 1, 1), plane)

    def center(fields, i, x):
        return fields[i, x + 1, TOP:TOP + ny, :]

    def ends(zr, i, x):
        return pltpu.roll(zr[0, i], nz - 1 - 2 * x, 1)

    def z_up(v, end):
        return jnp.where(last_lane, end, pltpu.roll(v, nz - 1, 1))

    def z_down(v, end):
        return jnp.where(first_lane, end, pltpu.roll(v, 1, 1))

    def around(fields, i, x, v, zr):
        end = ends(zr, i, x)
        return [
            z_up(v, end), z_down(v, end),
            fields[i, x + 2, TOP:TOP + ny, :], fields[i, x, TOP:TOP + ny, :],
            fields[i, x + 1, TOP + 1:TOP + 1 + ny, :], fields[i, x + 1, TOP - 1:TOP - 1 + ny, :],
        ]

    def total(terms):
        return functools.reduce(lambda p, q: p + q, terms)

    pairs = copies(0, f_in, ys_in, yr_in, zs_in, zr_in)
    for load in loads[:4]:
        load.wait()
    pack_rows(f_in, ys_in, 3)

    pl.semaphore_wait(barrier, sum(h.astype(jnp.int32) for h in has_lo + has_hi))

    start(pairs, 1)
    start(pairs, 0)

    blank = jnp.zeros((ny, nz), jnp.float32)

    def pack_in(x, planes):
        return tuple(pack_column(p, center(f_in, i, x), x) for i, p in enumerate(planes))

    planes = lax.fori_loop(0, nx, pack_in, (blank,) * 4, unroll=4)
    for i in range(4):
        zs_in[i] = planes[i]
    start(pairs, 2)

    sx, sy, sz = mask.shape
    weight[...] = jnp.zeros(weight.shape, jnp.float32)
    for i in range(sx):
        picked = jnp.zeros((sy, sz), jnp.float32)
        for c in range(class_weight.shape[0]):
            picked = picked + jnp.where(label[i] == c, class_weight[c], 0.0)
        weight[i * sy:(i + 1) * sy, 0:sz] = mask[i].astype(jnp.float32) * picked
    spread = (
        lax.broadcasted_iota(jnp.int32, (nz, nz), 0) == lax.broadcasted_iota(jnp.int32, (nz, nz), 1) // VOXEL
    ).astype(jnp.float32)
    weight[...] = jnp.dot(weight[...], spread, precision=EXACT, preferred_element_type=jnp.float32)
    for load in loads[4:]:
        load.wait()

    finish(pairs)
    unpack(f_in, yr_in, zr_in, 3)

    def first(x, planes):
        c, d, s, v = (center(f_in, i, x) for i in range(4))
        cn = around(f_in, 0, x, c, zr_in)
        dn = around(f_in, 1, x, d, zr_in)
        sn = around(f_in, 2, x, s, zr_in)
        v_down = z_down(v, ends(zr_in, 3, x))
        diff = [n - c for n in cn]
        g_d = total([(d + k) * q for k, q in zip(dn, diff)])
        g_s = total([(s + k) * q for k, q in zip(sn, diff)])
        rate = 0.5 * g_d + v_down * cn[1] - v * c
        inv = 1.0 / cap[x]
        r = time_step * inv
        cs = r * inv * capstep[x]
        later = c + r * rate
        tangent = 0.5 * r * g_s - cs * rate
        ratio[x] = r
        capstep[x] = cs
        rate1[x] = rate
        f_mid[0, x + 1, TOP:TOP + ny, :] = later
        f_mid[1, x + 1, TOP:TOP + ny, :] = tangent
        return pack_column(planes[0], later, x), pack_column(planes[1], tangent, x)

    planes = lax.fori_loop(0, nx, first, (blank,) * 2, unroll=2)
    pairs = copies(1, f_mid, ys_mid, yr_mid, zs_mid, zr_mid)
    pack_rows(f_mid, ys_mid, 2)
    start(pairs, 1)
    start(pairs, 0)
    zs_mid[0] = planes[0]
    zs_mid[1] = planes[1]
    start(pairs, 2)
    finish(pairs)
    unpack(f_mid, yr_mid, zr_mid, 2)

    def second_at(x):
        l, t = (center(f_mid, i, x) for i in range(2))
        d, s, v = (center(f_in, i, x) for i in range(1, 4))
        ln = around(f_mid, 0, x, l, zr_mid)
        tn = around(f_mid, 1, x, t, zr_mid)
        dn = around(f_in, 1, x, d, zr_in)
        sn = around(f_in, 2, x, s, zr_in)
        v_down = z_down(v, ends(zr_in, 3, x))
        l_diff = [n - l for n in ln]
        kd = [d + k for k in dn]
        rate = 0.5 * total([k * q for k, q in zip(kd, l_diff)]) + v_down * ln[1] - v * l
        mixed = total([k * (n - t) + (s + m) * q for k, n, m, q in zip(kd, tn, sn, l_diff)])
        rate2[x] = rate
        return t + ratio[x] * (0.5 * mixed + v_down * tn[1] - v * t) - capstep[x] * rate

    def voxel_row(g, carry):
        def one(i, acc):
            return acc + second_at(g * VOXEL + i)

        acc = lax.fori_loop(0, VOXEL, one, blank, unroll=2)
        sums = jnp.concatenate(
            [jnp.sum(acc[j * VOXEL:(j + 1) * VOXEL], axis=0, keepdims=True) for j in range(sy)], axis=0)
        coarse[pl.ds(g * sy, sy), :] = sums
        return carry

    lax.fori_loop(0, sx, voxel_row, 0)
    sums = coarse[...]
    wide = lax.broadcasted_iota(jnp.int32, sums.shape, 1)
    for hop in (1, 2, 4):
        sums = sums + jnp.where((wide & hop) == 0, pltpu.roll(sums, nz - hop, 1), pltpu.roll(sums, hop, 1))
    coarse[...] = weight[...] * (sums * (1.0 / VOXEL**3))

    def source_at(x):
        g = x // VOXEL
        return jnp.concatenate(
            [jnp.broadcast_to(coarse[pl.ds(g * sy + j, 1), :], (VOXEL, nz)) for j in range(sy)], axis=0)

    def scale(x, plane):
        scaled = ratio[x] * source_at(x)
        f_sc[0, x + 1, TOP:TOP + ny, :] = scaled
        return pack_column(plane, scaled, x)

    plane = lax.fori_loop(0, nx, scale, blank, unroll=4)
    pairs = copies(2, f_sc, ys_sc, yr_sc, zs_sc, zr_sc)
    pack_rows(f_sc, ys_sc, 1)
    start(pairs, 1)
    start(pairs, 0)
    zs_sc[0] = plane
    start(pairs, 2)
    finish(pairs)
    unpack(f_sc, yr_sc, zr_sc, 1)

    def third(x, plane):
        d, v = center(f_in, 1, x), center(f_in, 3, x)
        w = center(f_sc, 0, x)
        dn = around(f_in, 1, x, d, zr_in)
        wn = around(f_sc, 0, x, w, zr_sc)
        g = total([(d + k) * (n - w) for k, n in zip(dn, wn)])
        earlier = source_at(x) + 0.5 * g + v * (wn[0] - w)
        r = ratio[x]
        one = r * earlier
        f_first[0, x + 1, TOP:TOP + ny, :] = one
        return pack_column(plane, one, x)

    plane = lax.fori_loop(0, nx, third, blank, unroll=2)
    pairs = copies(3, f_first, ys_first, yr_first, zs_first, zr_first)
    pack_rows(f_first, ys_first, 1)
    start(pairs, 1)
    start(pairs, 0)
    zs_first[0] = plane
    start(pairs, 2)

    def fourth(x, carry):
        w = center(f_sc, 0, x)
        l = center(f_mid, 0, x)
        one = center(f_first, 0, x)
        wn = around(f_sc, 0, x, w, zr_sc)
        ln = around(f_mid, 0, x, l, zr_mid)
        part[x] = total([(w - m) * (n - l) for m, n in zip(wn, ln)])
        res_c[x] = -(w * rate2[x] + one * rate1[x]) * (ratio[x] * (1.0 / time_step))
        return carry

    lax.fori_loop(0, nx, fourth, 0, unroll=2)
    store_c = pltpu.make_async_copy(res_c, out_c, out_sem.at[0])
    store_c.start()
    finish(pairs)
    unpack(f_first, yr_first, zr_first, 1)

    def fifth(x, carry):
        one = center(f_first, 0, x)
        c = center(f_in, 0, x)
        on = around(f_first, 0, x, one, zr_first)
        cn = around(f_in, 0, x, c, zr_in)
        res_d[x] = 0.5 * (part[x] + total([(one - m) * (n - c) for m, n in zip(on, cn)]))
        return carry

    lax.fori_loop(0, nx, fifth, 0, unroll=2)
    store_d = pltpu.make_async_copy(res_d, out_d, out_sem.at[1])
    store_d.start()
    store_c.wait()
    store_d.wait()


def shards(concentration, dispersion, disp_step, capacity, cap_step, velocity, voxel_mask, voxel_class, class_weight):
    nx, ny, nz = concentration.shape
    f32 = jnp.float32
    block = jax.ShapeDtypeStruct((nx, ny, nz), f32)
    hbm = pl.BlockSpec(memory_space=pl.ANY)
    vmem = pl.BlockSpec(memory_space=pltpu.VMEM)
    smem = pl.BlockSpec(memory_space=pltpu.SMEM)
    whole = pltpu.VMEM((nx, ny, nz), f32)
    coarse_rows = -(-(nx // VOXEL) * (ny // VOXEL) // 8) * 8
    per_phase = (3, 2, 1, 1)
    z_phase = (4, 2, 1, 1)
    fields = (4, 2, 1, 1)
    scratch = (
        [pltpu.VMEM((k, nx + 2, ny + 2 * EDGE, nz), f32) for k in fields]
        + [whole] * 8
        + [pltpu.VMEM((2, k, nx, nz), f32) for k in per_phase]
        + [pltpu.VMEM((2, k, nx, nz), f32) for k in per_phase]
        + [pltpu.VMEM((k, ny, nz), f32) for k in z_phase]
        + [pltpu.VMEM((2, k, ny, nz), f32) for k in z_phase]
        + [pltpu.VMEM((coarse_rows, nz), f32)] * 2
        + [pltpu.SemaphoreType.DMA((6,)), pltpu.SemaphoreType.DMA((2,))]
        + [pltpu.SemaphoreType.DMA((24,))] * 2
    )
    return pl.pallas_call(
        kernel,
        out_shape=(block, block),
        in_specs=[hbm] * 6 + [vmem, vmem, smem],
        out_specs=(hbm, hbm),
        scratch_shapes=scratch,
        compiler_params=pltpu.CompilerParams(
            collective_id=0, has_side_effects=True, vmem_limit_bytes=32 * 1024 * 1024),
    )(concentration, dispersion, disp_step, velocity, capacity, cap_step, voxel_mask, voxel_class, class_weight)


def solution(mesh):
    cube = P("gx", "gy", "gz")
    return jax.shard_map(
        shards, mesh=mesh, in_specs=(cube,) * 8 + (P(),), out_specs=(cube, cube), check_vma=False)
```

```python
import functools

import jax
import jax.numpy as jnp
from jax import lax
from jax.experimental import pallas as pl
from jax.experimental.pallas import tpu as pltpu
from jax.sharding import PartitionSpec as P

time_step = 0.1
MESH = pl.DeviceIdType.MESH
AXES = ("gx", "gy", "gz")
TOP = 8
EDGE = 8
VOXEL = 8
EXACT = lax.Precision.HIGHEST


def kernel(
    conc, disp, step, vel, cap_in, capstep_in, mask_in, label_in, class_weight,
    out_d, out_c,
    f_in, f_mid, f_sc, f_first,
    mask, label, up_in, up_mid, up_sc, up_first, down_in, down_mid, down_sc, down_first,
    cap, capstep, ratio, rate1, rate2, part, res_d, res_c,
    ys_in, ys_mid, ys_sc, ys_first,
    yr_in, yr_mid, yr_sc, yr_first,
    zs_in, zs_mid, zs_sc, zs_first,
    zr_in, zr_mid, zr_sc, zr_first,
    coarse, weight, load_sem, out_sem, send_sem, recv_sem,
):
    nx, ny, nz = cap.shape
    rows = ny + 2 * EDGE
    place = [lax.axis_index(a) for a in AXES]
    count = [lax.axis_size(a) for a in AXES]
    has_lo = [p > 0 for p in place]
    has_hi = [p < n - 1 for p, n in zip(place, count)]

    def main(ref):
        return ref.at[pl.ds(1, nx), pl.ds(TOP, ny)]

    loads = []
    for i, (src, dst) in enumerate((
        (conc, main(f_in.at[0])), (disp, main(f_in.at[1])), (step, main(f_in.at[2])),
        (vel, main(f_in.at[3])), (cap_in, cap), (capstep_in, capstep), (mask_in, mask), (label_in, label),
    )):
        load = pltpu.make_async_copy(src, dst, load_sem.at[i])
        load.start()
        loads.append(load)

    for ref in (f_in, f_mid, f_sc, f_first):
        for k in range(ref.shape[0]):
            for x in (0, nx + 1):
                ref[k, x, TOP:TOP + ny, :] = jnp.zeros((ny, nz), jnp.float32)
    for ref in (yr_in, yr_mid, yr_sc, yr_first, zr_in, zr_mid, zr_sc, zr_first):
        ref[...] = jnp.zeros(ref.shape, jnp.float32)

    barrier = pltpu.get_barrier_semaphore()
    for a, name in enumerate(AXES):
        @pl.when(has_lo[a])
        def _():
            pl.semaphore_signal(barrier, inc=1, device_id={name: place[a] - 1}, device_id_type=MESH)

        @pl.when(has_hi[a])
        def _():
            pl.semaphore_signal(barrier, inc=1, device_id={name: place[a] + 1}, device_id_type=MESH)

    lane = lax.broadcasted_iota(jnp.int32, (ny, nz), 1)
    first_lane = lane == 0
    last_lane = lane == nz - 1
    pair = lane // 2

    def copies(phase, fields, ys, yr, zs, zr):
        k = yr.shape[1]

        def remote(src, dst, axis, side):
            at = (phase * 3 + axis) * 2 + side
            to = place[axis] - 1 if side == 0 else place[axis] + 1
            return pltpu.make_async_remote_copy(
                src_ref=src, dst_ref=dst, send_sem=send_sem.at[at], recv_sem=recv_sem.at[at],
                device_id={AXES[axis]: to}, device_id_type=MESH)

        def slab(x):
            return fields.at[pl.ds(0, k), x, pl.ds(TOP, ny)]

        return [
            (remote(slab(1), slab(nx + 1), 0, 0), remote(slab(nx), slab(0), 0, 1)),
            (remote(ys.at[0], yr.at[1], 1, 0), remote(ys.at[1], yr.at[0], 1, 1)),
            (remote(zs, zr.at[1], 2, 0), remote(zs, zr.at[0], 2, 1)),
        ]

    def start(pairs, axis):
        lo, hi = pairs[axis]

        @pl.when(has_lo[axis])
        def _():
            lo.start()

        @pl.when(has_hi[axis])
        def _():
            hi.start()

    def finish(pairs):
        for axis in range(3):
            lo, hi = pairs[axis]

            @pl.when(has_lo[axis])
            def _():
                hi.wait_recv()
                lo.wait_send()

            @pl.when(has_hi[axis])
            def _():
                lo.wait_recv()
                hi.wait_send()

    def pack_rows(fields, ys, k):
        flat = fields.reshape(fields.shape[0], (nx + 2) * rows, nz)
        for i in range(k):
            ys[0, i] = flat[i, pl.ds(rows + TOP, nx, stride=rows), :]
            ys[1, i] = flat[i, pl.ds(rows + TOP + ny - 1, nx, stride=rows), :]

    def unpack(fields, yr, zr, k):
        flat = fields.reshape(fields.shape[0], (nx + 2) * rows, nz)
        for i in range(k):
            flat[i, pl.ds(rows + TOP - 1, nx, stride=rows), :] = yr[0, i]
            flat[i, pl.ds(rows + TOP + ny, nx, stride=rows), :] = yr[1, i]
        for i in range(zr.shape[1]):
            above = pltpu.roll(zr[1, i], nz - 1, 1)
            below = pltpu.roll(zr[0, i], 1, 1)
            zr[0, i] = jnp.where(lane % 2 == 0, above, below)

    def pack_column(plane, slab, x):
        return jnp.where(pair == x, pltpu.roll(slab, 2 * x + 1, 1), plane)

    def center(fields, i, x):
        return fields[i, x + 1, TOP:TOP + ny, :]

    def shift(fields, up, down, k_up, k_down):
        def one(x, carry):
            for i in range(k_down):
                v = center(fields, i, x)
                down[i, x] = pltpu.roll(v, 1, 1)
                if i < k_up:
                    up[i, x] = pltpu.roll(v, nz - 1, 1)
            return carry

        lax.fori_loop(0, nx, one, 0, unroll=8)

    def patch(zr, up, down, k_up, k_down):
        def one(x, carry):
            for i in range(k_down):
                end = pltpu.roll(zr[0, i], nz - 1 - 2 * x, 1)
                pltpu.store(down.at[i, x], end, mask=first_lane)
                if i < k_up:
                    pltpu.store(up.at[i, x], end, mask=last_lane)
            return carry

        lax.fori_loop(0, nx, one, 0, unroll=8)

    def pack(fields, zs, k):
        def one(x, planes):
            return tuple(pack_column(p, center(fields, i, x), x) for i, p in enumerate(planes))

        planes = lax.fori_loop(0, nx, one, (jnp.zeros((ny, nz), jnp.float32),) * k, unroll=8)
        for i in range(k):
            zs[i] = planes[i]

    def around(fields, i, x, up, down):
        return [
            up[i, x], down[i, x],
            fields[i, x + 2, TOP:TOP + ny, :], fields[i, x, TOP:TOP + ny, :],
            fields[i, x + 1, TOP + 1:TOP + 1 + ny, :], fields[i, x + 1, TOP - 1:TOP - 1 + ny, :],
        ]

    def total(terms):
        return functools.reduce(lambda p, q: p + q, terms)

    pairs = copies(0, f_in, ys_in, yr_in, zs_in, zr_in)
    for load in loads[:4]:
        load.wait()
    pack_rows(f_in, ys_in, 3)

    pl.semaphore_wait(barrier, sum(h.astype(jnp.int32) for h in has_lo + has_hi))

    start(pairs, 1)
    start(pairs, 0)

    blank = jnp.zeros((ny, nz), jnp.float32)

    pack(f_in, zs_in, 4)
    start(pairs, 2)
    shift(f_in, up_in, down_in, 3, 4)
    for load in loads[4:]:
        load.wait()

    def prepare(x, carry):
        inv = 1.0 / cap[x]
        r = time_step * inv
        ratio[x] = r
        capstep[x] = r * inv * capstep[x]
        return carry

    lax.fori_loop(0, nx, prepare, 0, unroll=4)

    sx, sy, sz = mask.shape
    weight[...] = jnp.zeros(weight.shape, jnp.float32)
    for i in range(sx):
        picked = jnp.zeros((sy, sz), jnp.float32)
        for c in range(class_weight.shape[0]):
            picked = picked + jnp.where(label[i] == c, class_weight[c], 0.0)
        weight[i * sy:(i + 1) * sy, 0:sz] = mask[i].astype(jnp.float32) * picked
    spread = (
        lax.broadcasted_iota(jnp.int32, (nz, nz), 0) == lax.broadcasted_iota(jnp.int32, (nz, nz), 1) // VOXEL
    ).astype(jnp.float32)
    weight[...] = jnp.dot(weight[...], spread, precision=EXACT, preferred_element_type=jnp.float32)
    finish(pairs)
    unpack(f_in, yr_in, zr_in, 3)
    patch(zr_in, up_in, down_in, 3, 4)

    def first(x, carry):
        c, d, s, v = (center(f_in, i, x) for i in range(4))
        cn = around(f_in, 0, x, up_in, down_in)
        dn = around(f_in, 1, x, up_in, down_in)
        sn = around(f_in, 2, x, up_in, down_in)
        v_down = down_in[3, x]
        diff = [n - c for n in cn]
        g_d = total([(d + k) * q for k, q in zip(dn, diff)])
        g_s = total([(s + k) * q for k, q in zip(sn, diff)])
        rate = 0.5 * g_d + v_down * cn[1] - v * c
        r = ratio[x]
        cs = capstep[x]
        later = c + r * rate
        tangent = 0.5 * r * g_s - cs * rate
        rate1[x] = rate
        f_mid[0, x + 1, TOP:TOP + ny, :] = later
        f_mid[1, x + 1, TOP:TOP + ny, :] = tangent
        return carry

    lax.fori_loop(0, nx, first, 0, unroll=4)
    pairs = copies(1, f_mid, ys_mid, yr_mid, zs_mid, zr_mid)
    pack_rows(f_mid, ys_mid, 2)
    start(pairs, 1)
    start(pairs, 0)
    pack(f_mid, zs_mid, 2)
    start(pairs, 2)
    shift(f_mid, up_mid, down_mid, 2, 2)
    finish(pairs)
    unpack(f_mid, yr_mid, zr_mid, 2)
    patch(zr_mid, up_mid, down_mid, 2, 2)

    def second_at(x):
        l, t = (center(f_mid, i, x) for i in range(2))
        d, s, v = (center(f_in, i, x) for i in range(1, 4))
        ln = around(f_mid, 0, x, up_mid, down_mid)
        tn = around(f_mid, 1, x, up_mid, down_mid)
        dn = around(f_in, 1, x, up_in, down_in)
        sn = around(f_in, 2, x, up_in, down_in)
        v_down = down_in[3, x]
        l_diff = [n - l for n in ln]
        kd = [d + k for k in dn]
        rate = 0.5 * total([k * q for k, q in zip(kd, l_diff)]) + v_down * ln[1] - v * l
        mixed = total([k * (n - t) + (s + m) * q for k, n, m, q in zip(kd, tn, sn, l_diff)])
        rate2[x] = rate
        return t + ratio[x] * (0.5 * mixed + v_down * tn[1] - v * t) - capstep[x] * rate

    def voxel_row(g, carry):
        def one(i, acc):
            return acc + second_at(g * VOXEL + i)

        acc = lax.fori_loop(0, VOXEL, one, blank, unroll=4)
        sums = jnp.concatenate(
            [jnp.sum(acc[j * VOXEL:(j + 1) * VOXEL], axis=0, keepdims=True) for j in range(sy)], axis=0)
        coarse[pl.ds(g * sy, sy), :] = sums
        return carry

    lax.fori_loop(0, sx, voxel_row, 0)
    sums = coarse[...]
    wide = lax.broadcasted_iota(jnp.int32, sums.shape, 1)
    for hop in (1, 2, 4):
        sums = sums + jnp.where((wide & hop) == 0, pltpu.roll(sums, nz - hop, 1), pltpu.roll(sums, hop, 1))
    coarse[...] = weight[...] * (sums * (1.0 / VOXEL**3))

    def source_at(x):
        g = x // VOXEL
        return jnp.concatenate(
            [jnp.broadcast_to(coarse[pl.ds(g * sy + j, 1), :], (VOXEL, nz)) for j in range(sy)], axis=0)

    def scale(x, carry):
        scaled = ratio[x] * source_at(x)
        f_sc[0, x + 1, TOP:TOP + ny, :] = scaled
        return carry

    lax.fori_loop(0, nx, scale, 0, unroll=8)
    pairs = copies(2, f_sc, ys_sc, yr_sc, zs_sc, zr_sc)
    pack_rows(f_sc, ys_sc, 1)
    start(pairs, 1)
    start(pairs, 0)
    pack(f_sc, zs_sc, 1)
    start(pairs, 2)
    shift(f_sc, up_sc, down_sc, 1, 1)
    finish(pairs)
    unpack(f_sc, yr_sc, zr_sc, 1)
    patch(zr_sc, up_sc, down_sc, 1, 1)

    def third(x, carry):
        d, v = center(f_in, 1, x), center(f_in, 3, x)
        w = center(f_sc, 0, x)
        dn = around(f_in, 1, x, up_in, down_in)
        wn = around(f_sc, 0, x, up_sc, down_sc)
        g = total([(d + k) * (n - w) for k, n in zip(dn, wn)])
        earlier = source_at(x) + 0.5 * g + v * (wn[0] - w)
        r = ratio[x]
        one = r * earlier
        f_first[0, x + 1, TOP:TOP + ny, :] = one
        return carry

    lax.fori_loop(0, nx, third, 0, unroll=4)
    pairs = copies(3, f_first, ys_first, yr_first, zs_first, zr_first)
    pack_rows(f_first, ys_first, 1)
    start(pairs, 1)
    start(pairs, 0)
    pack(f_first, zs_first, 1)
    start(pairs, 2)
    shift(f_first, up_first, down_first, 1, 1)

    def fourth(x, carry):
        w = center(f_sc, 0, x)
        l = center(f_mid, 0, x)
        one = center(f_first, 0, x)
        wn = around(f_sc, 0, x, up_sc, down_sc)
        ln = around(f_mid, 0, x, up_mid, down_mid)
        part[x] = total([(w - m) * (n - l) for m, n in zip(wn, ln)])
        res_c[x] = -(w * rate2[x] + one * rate1[x]) * (ratio[x] * (1.0 / time_step))
        return carry

    lax.fori_loop(0, nx, fourth, 0, unroll=4)
    store_c = pltpu.make_async_copy(res_c, out_c, out_sem.at[0])
    store_c.start()
    finish(pairs)
    unpack(f_first, yr_first, zr_first, 1)
    patch(zr_first, up_first, down_first, 1, 1)

    def fifth(x, carry):
        one = center(f_first, 0, x)
        c = center(f_in, 0, x)
        on = around(f_first, 0, x, up_first, down_first)
        cn = around(f_in, 0, x, up_in, down_in)
        res_d[x] = 0.5 * (part[x] + total([(one - m) * (n - c) for m, n in zip(on, cn)]))
        return carry

    lax.fori_loop(0, nx, fifth, 0, unroll=4)
    store_d = pltpu.make_async_copy(res_d, out_d, out_sem.at[1])
    store_d.start()
    store_c.wait()
    store_d.wait()


def shards(concentration, dispersion, disp_step, capacity, cap_step, velocity, voxel_mask, voxel_class, class_weight):
    nx, ny, nz = concentration.shape
    f32 = jnp.float32
    block = jax.ShapeDtypeStruct((nx, ny, nz), f32)
    hbm = pl.BlockSpec(memory_space=pltpu.HBM)
    smem = pl.BlockSpec(memory_space=pltpu.SMEM)
    whole = pltpu.VMEM((nx, ny, nz), f32)
    coarse_rows = -(-(nx // VOXEL) * (ny // VOXEL) // 8) * 8
    per_phase = (3, 2, 1, 1)
    z_phase = (4, 2, 1, 1)
    fields = (4, 2, 1, 1)
    scratch = (
        [pltpu.VMEM((k, nx + 2, ny + 2 * EDGE, nz), f32) for k in fields]
        + [pltpu.VMEM(voxel_mask.shape, jnp.int32)] * 2
        + [pltpu.VMEM((k, nx, ny, nz), f32) for k in fields]
        + [pltpu.VMEM((k, nx, ny, nz), f32) for k in fields]
        + [whole] * 8
        + [pltpu.VMEM((2, k, nx, nz), f32) for k in per_phase]
        + [pltpu.VMEM((2, k, nx, nz), f32) for k in per_phase]
        + [pltpu.VMEM((k, ny, nz), f32) for k in z_phase]
        + [pltpu.VMEM((2, k, ny, nz), f32) for k in z_phase]
        + [pltpu.VMEM((coarse_rows, nz), f32)] * 2
        + [pltpu.SemaphoreType.DMA((8,)), pltpu.SemaphoreType.DMA((2,))]
        + [pltpu.SemaphoreType.DMA((24,))] * 2
    )
    return pl.pallas_call(
        kernel,
        out_shape=(block, block),
        in_specs=[hbm] * 8 + [smem],
        out_specs=(hbm, hbm),
        scratch_shapes=scratch,
        compiler_params=pltpu.CompilerParams(
            collective_id=0, has_side_effects=True, vmem_limit_bytes=32 * 1024 * 1024),
    )(concentration, dispersion, disp_step, velocity, capacity, cap_step, voxel_mask, voxel_class, class_weight)


def solution(mesh):
    cube = P("gx", "gy", "gz")
    return jax.shard_map(
        shards, mesh=mesh, in_specs=(cube,) * 8 + (P(),), out_specs=(cube, cube), check_vma=False)
```
